32 devices in a mesh: grp: 2 (over x), ta: 16 (over z, y, core).
Axes of the slice: x: 2, y: 2, z: 4, core: 2. Of those that a mesh axis runs over, the one named last changes fastest.
Arguments:
- frames_in: bfloat16 [32, 16, 128, 256], P(('grp', 'ta')), parts along dimension 0, may hold values from -6 to 6
- cotangent: bfloat16 [32, 16, 128, 256], P(('grp', 'ta')), parts along dimension 0, may hold values from -6 to 6
- spatial_w: bfloat16 [3, 3, 256, 256], replicated, may hold values from -0.125 to 0.125
- temporal_w: bfloat16 [3, 256, 256], replicated, may hold values from -0.21875 to 0.21875
Outputs:
- input_grad: bfloat16 [32, 16, 128, 256], P(('grp', 'ta')), parts along dimension 0
- spatial_grad: float32 [4608, 256], P(('grp', 'ta')), parts along dimension 0
- temporal_grad: float32 [1536, 256], P(('grp', 'ta')), parts along dimension 0
The draws below stay inside these ranges and needn't reach their ends.
There are 2 independent parts, one for each index of `grp`. The reference program is written for one: setup_inputs(seed, part) draws one part's arguments, and reference() takes and returns one part's arrays. A program takes and returns all parts, laid end to end along the dimension named above; an argument that names none is the same for every part. Nothing has to cross between parts.
All inputs are finite; a program needn't handle non-finite values.
Results may differ from the reference program's by a relative error of at most 0.0031.
Values may be sent and summed in bfloat16 or wider, within the bound.
A program may use at most 64 MiB of HBM per device.

```python
import math
import jax
import jax.numpy as jnp

C = 256
H = 16
W = 128
TAP_DILATION = 1
FRAMES = 16


def level_of(rng, extent, pieces, smallest, top_value):
    def one(position, blocks):
        draws = jax.random.uniform(jax.random.fold_in(jax.random.fold_in(rng, 6), position), (blocks,), jnp.float32, smallest / len(pieces), top_value / len(pieces))
        return jnp.repeat(jnp.exp(draws), extent[position] // blocks).reshape((-1,) + (1,) * (len(extent) - position - 1))

    gain = one(*pieces[0])
    for cut in pieces[1:]:
        gain = gain * one(*cut)
    return gain


def bell_draw(own_key, shape, scale, reach, pieces=(), held_as=jnp.bfloat16):
    result = scale * jax.random.normal(own_key, shape, jnp.float32)
    if pieces:
        result = result * level_of(own_key, shape, pieces, -0.22, 0.18)
    return jnp.clip(result, -reach, reach).astype(held_as)


def setup_inputs(seed: int = 0, part: int = 0) -> dict:
    key_of = jax.random.split(jax.random.key(seed), 5)
    own_keys = jax.random.split(jax.random.fold_in(key_of[4], part), 5)
    return {
        "frames_in": bell_draw(own_keys[0], (FRAMES, H, W, C), 1.0, 6.0, ((0, 16),)),
        "cotangent": bell_draw(own_keys[1], (FRAMES, H, W, C), 1.0, 6.0, ((0, 16),)),
        "spatial_w": bell_draw(key_of[2], (3, 3, C, C), (9 * C) ** -0.5, 0.125),
        "temporal_w": bell_draw(key_of[3], (3, C, C), (3 * C) ** -0.5, 0.21875),
    }


def backward_shifted(field, lag):
    frames = field.shape[0]
    padded = jnp.pad(field, ((lag, 0), (0, 0), (0, 0), (0, 0)))
    return padded[:frames]

def forward_shifted(field, lag):
    padded = jnp.pad(field, ((0, lag), (0, 0), (0, 0), (0, 0)))
    return padded[lag:]

def reference(frames_in, cotangent, spatial_w, temporal_w):
    input_frames = frames_in.astype(jnp.float32)
    upstream = cotangent.astype(jnp.float32)
    spatial = spatial_w.astype(jnp.float32)
    temporal_conv = temporal_w.astype(jnp.float32)
    frames, rows, cols = (input_frames.shape[0], input_frames.shape[1], input_frames.shape[2])
    g_scale = 1.0 / math.sqrt(frames * rows * cols)
    preactivation = jnp.zeros(input_frames.shape, jnp.float32)
    for tap_number in range(3):
        preactivation = preactivation + jnp.einsum('iqgv,vx->iqgx', backward_shifted(input_frames, tap_number * TAP_DILATION), temporal_conv[tap_number])
    act = jax.nn.silu(preactivation).astype(jnp.bfloat16)
    act_wide = act.astype(jnp.float32)
    up_pad = jnp.pad(upstream, ((0, 0), (1, 1), (1, 1), (0, 0)))
    act_pad = jnp.pad(act_wide, ((0, 0), (1, 1), (1, 1), (0, 0)))
    act_grad = jnp.zeros(input_frames.shape, jnp.float32)
    blocks = []
    for row_i in range(3):
        for col_j in range(3):
            piece = up_pad[:, 2 - row_i:2 - row_i + rows, 2 - col_j:2 - col_j + cols]
            act_grad = act_grad + jnp.einsum('oxzu,iu->oxzi', piece, spatial[row_i, col_j])
            moved = act_pad[:, row_i:row_i + rows, col_j:col_j + cols]
            blocks.append(jnp.einsum('krsv,krsn->vn', moved, upstream))
    spatial_grad = jnp.concatenate(blocks, axis=0) * g_scale
    sigmoid_v = jax.nn.sigmoid(preactivation)
    v_grad = (act_grad * sigmoid_v * (1.0 + preactivation * (1.0 - sigmoid_v))).astype(jnp.bfloat16)
    value_extended = v_grad.astype(jnp.float32)
    temporal_layers = []
    temporal_adjoint = jnp.zeros(input_frames.shape, jnp.float32)
    for tap_number in range(3):
        temporal_layers.append(jnp.einsum('krsv,krsn->vn', backward_shifted(input_frames, tap_number * TAP_DILATION), value_extended))
        temporal_adjoint = temporal_adjoint + jnp.einsum('oxzu,iu->oxzi', forward_shifted(value_extended, tap_number * TAP_DILATION), temporal_conv[tap_number])
    temporal_grad = jnp.concatenate(temporal_layers, axis=0) * g_scale
    input_grad = (upstream + temporal_adjoint).astype(jnp.bfloat16)
    return (input_grad, spatial_grad, temporal_grad)
```

```python
import functools
import math

import jax
import jax.numpy as jnp
from jax import lax
from jax.experimental import pallas as pl
from jax.experimental.pallas import tpu as pltpu
from jax.sharding import PartitionSpec as P

F32, BF16 = jnp.float32, jnp.bfloat16
CHUNKS = 4
LAG = 4


def dot(a, b):
    return jnp.dot(a, b, preferred_element_type=F32)


def dot_t(a, b):
    return lax.dot_general(a, b, (((1,), (1,)), ((), ())), preferred_element_type=F32)


def kernel(
    n, cells, cols, chans, fused, g_scale,
    x_hbm, cot_hbm, sw_hbm, tw_hbm, *rest,
):
    if fused:
        out_hbm, sg_hbm, tg_hbm = rest[:3]
    else:
        out_hbm, sg_hbm, tg_hbm = rest[:3]
    (cotp, sw, tw, xs, vgs, agrad, act_t, x_t, s_sum, t_sum, out_v,
     local_sem, out_sem, xsend, xfwd, xrecv, vsend, vfwd, vrecv) = rest[3:22]
    me = lax.axis_index("ta")
    core = lax.rem(me, 2)
    even = core == 0
    size = cells // CHUNKS

    def rows(k):
        return pl.ds(pl.multiple_of(k * size, size), size)

    def remote(src, dst, ssem, rsem, to):
        return pltpu.make_async_remote_copy(
            src_ref=src, dst_ref=dst, send_sem=ssem, recv_sem=rsem,
            device_id={"ta": to}, device_id_type=pl.DeviceIdType.MESH,
        )

    steps = [1, 2, n - 1, n - 2]
    if fused:
        steps += [4, 8, 12]
    barrier = pltpu.get_barrier_semaphore()
    for step in steps:
        pl.semaphore_signal(
            barrier, inc=1, device_id={"ta": lax.rem(me + step, n)},
            device_id_type=pl.DeviceIdType.MESH,
        )
    loads = [
        pltpu.make_async_copy(cot_hbm, cotp.at[1, pl.ds(cols, cells)], local_sem.at[0]),
        pltpu.make_async_copy(sw_hbm, sw, local_sem.at[1]),
        pltpu.make_async_copy(x_hbm, xs.at[0], local_sem.at[2]),
        pltpu.make_async_copy(tw_hbm, tw, local_sem.at[3]),
    ]
    for load in loads:
        load.start()
    pl.semaphore_wait(barrier, len(steps))

    def x_one(k):
        return remote(x_hbm.at[rows(k)], xs.at[1, rows(k)], xsend.at[0, k], xrecv.at[0, k],
                      lax.rem(me + 1, n))

    def x_two(k):
        return remote(x_hbm.at[rows(k)], xs.at[2, rows(k)], xsend.at[1, k], xrecv.at[1, k],
                      lax.rem(me + 2, n))

    def x_pass(k):
        return remote(xs.at[1, rows(k)], xs.at[2, rows(k)], xfwd.at[k], xrecv.at[1, k],
                      lax.rem(me + 1, n))

    def v_one(k):
        return remote(vgs.at[0, rows(k)], vgs.at[1, rows(k)], vsend.at[0, k], vrecv.at[0, k],
                      lax.rem(me + n - 1, n))

    def v_two(k):
        return remote(vgs.at[0, rows(k)], vgs.at[2, rows(k)], vsend.at[1, k], vrecv.at[1, k],
                      lax.rem(me + n - 2, n))

    def v_pass(k):
        return remote(vgs.at[1, rows(k)], vgs.at[2, rows(k)], vfwd.at[k], vrecv.at[1, k],
                      lax.rem(me + n - 1, n))

    x_has_one, x_has_two = me < n - 1, jnp.logical_and(even, me < n - 2)
    x_has_pass = jnp.logical_and(even, me >= 2)
    v_has_one, v_has_two = me >= 1, jnp.logical_and(core == 1, me >= 2)
    v_has_pass = jnp.logical_and(core == 1, me < n - 1)

    for k in range(CHUNKS):
        @pl.when(x_has_one)
        def _():
            x_one(k).start()

        @pl.when(x_has_two)
        def _():
            x_two(k).start()

    @pl.when(me == 0)
    def _():
        xs[1] = jnp.zeros((cells, chans), BF16)

    @pl.when(me < 2)
    def _():
        xs[2] = jnp.zeros((cells, chans), BF16)

    @pl.when(me == n - 1)
    def _():
        vgs[1] = jnp.zeros((cells, chans), BF16)

    @pl.when(me >= n - 2)
    def _():
        vgs[2] = jnp.zeros((cells, chans), BF16)

    edge = jnp.zeros((cols, chans), BF16)
    for j in range(3):
        cotp[j, pl.ds(0, cols)] = edge
        cotp[j, pl.ds(cols + cells, cols)] = edge
    loads[0].wait()

    def shift(k, carry):
        at = pl.ds(pl.multiple_of(cols + k * size, cols), size)
        piece = cotp[1, at].astype(F32)
        col = lax.rem(lax.broadcasted_iota(jnp.int32, (size, chans), 0), cols)
        cotp[0, at] = jnp.where(col == cols - 1, 0.0, pltpu.roll(piece, size - 1, 0)).astype(BF16)
        cotp[2, at] = jnp.where(col == 0, 0.0, pltpu.roll(piece, 1, 0)).astype(BF16)
        return carry

    lax.fori_loop(0, CHUNKS, shift, 0)
    loads[1].wait()

    def cot_at(k, i, j):
        return cotp[j, pl.ds(pl.multiple_of(k * size + (2 - i) * cols, cols), size)]

    def adjoint(k, carry):
        total = jnp.zeros((size, chans), F32)
        for i in range(3):
            for j in range(3):
                total = total + dot_t(cot_at(k, i, j), sw[i, j])
        agrad[rows(k)] = total
        return carry

    lax.fori_loop(0, CHUNKS, adjoint, 0)
    loads[2].wait()
    loads[3].wait()
    s_sum[...] = jnp.zeros_like(s_sum)
    t_sum[...] = jnp.zeros_like(t_sum)

    def send_v(k):
        @pl.when(v_has_one)
        def _():
            v_one(k).start()

        @pl.when(v_has_two)
        def _():
            v_two(k).start()

    def forward(k, carry):
        @pl.when(me >= 1)
        def _():
            x_one(k).wait_recv()

        @pl.when(x_has_pass)
        def _():
            x_pass(k).start()

        @pl.when(me >= 2)
        def _():
            x_two(k).wait_recv()

        at = rows(k)
        v = dot(xs[0, at], tw[0]) + dot(xs[1, at], tw[1]) + dot(xs[2, at], tw[2])
        s = 1.0 / (1.0 + jnp.exp(-v))
        vg = (agrad[at] * s * (1.0 + v * (1.0 - s))).astype(BF16)
        vgs[0, at] = vg
        act_t[...] = (v * s).astype(BF16).T
        if LAG < CHUNKS:
            @pl.when(k >= LAG)
            def _():
                send_v(k - LAG)
        for tap in range(3):
            x_t[tap * chans : (tap + 1) * chans] = xs[tap, at].T
        t_sum[...] += dot(x_t[...], vgs[0, at])
        for i in range(3):
            for j in range(3):
                block = pl.ds((3 * i + j) * chans, chans)
                s_sum[block] += dot(act_t[...], cot_at(k, i, j))
        return carry

    lax.fori_loop(0, CHUNKS, forward, 0)
    for k in range(max(CHUNKS - LAG, 0), CHUNKS):
        send_v(k)

    def back(k):
        @pl.when(me < n - 1)
        def _():
            v_one(k).wait_recv()

        @pl.when(v_has_pass)
        def _():
            v_pass(k).start()

        at = rows(k)
        total = dot_t(vgs[0, at], tw[0]) + dot_t(vgs[1, at], tw[1])

        @pl.when(me < n - 2)
        def _():
            v_two(k).wait_recv()

        total = total + dot_t(vgs[2, at], tw[2])
        cot = cotp[1, pl.ds(pl.multiple_of(cols + k * size, cols), size)].astype(F32)
        out_v[at] = (cot + total).astype(BF16)
        pltpu.make_async_copy(out_v.at[at], out_hbm.at[at], out_sem.at[k]).start()

    if fused:
        (send1, recv1, send2, recv2, send3, recv3, sg, tg,
         sem1, rsem1, sem2, rsem2, sem3, rsem3) = rest[22:]
        z = me // 4
        y = lax.rem(me // 2, 2)
        sr = 9 * chans // n
        tr = 3 * chans // n

        def own(b):
            return (s_sum[pl.ds(pl.multiple_of(sr * b, 16), sr)],
                    t_sum[pl.ds(pl.multiple_of(tr * b, 16), tr)])

        stage1 = []
        for part in range(2):
            to_y = 1 - y if part == 0 else y
            for zz in range(4):
                a, b = own(4 * zz + 2 * to_y + (1 - core))
                send1[part, zz, 0:sr] = a.astype(BF16)
                send1[part, zz, sr : sr + tr] = b.astype(BF16)
            copy = remote(send1.at[part], recv1.at[part], sem1.at[part], rsem1.at[part],
                          me + 1 - 2 * core)
            copy.start()
            stage1.append(copy)
        stage1[0].wait_recv()
        for zz in range(4):
            a, b = own(4 * zz + 2 * (1 - y) + core)
            send2[zz, 0:sr] = (a + recv1[0, zz, 0:sr].astype(F32)).astype(BF16)
            send2[zz, sr : sr + tr] = (b + recv1[0, zz, sr : sr + tr].astype(F32)).astype(BF16)
        stage2 = remote(send2, recv2, sem2.at[0], rsem2.at[0], me + 2 - 4 * y)
        stage2.start()
        half = CHUNKS // 2
        for k in range(half):
            back(k)
        stage1[1].wait_recv()
        stage2.wait_recv()

        def sum2(zz):
            a, b = own(4 * zz + 2 * y + core)
            a = a + recv1[1, zz, 0:sr].astype(F32) + recv2[zz, 0:sr].astype(F32)
            b = (b + recv1[1, zz, sr : sr + tr].astype(F32)
                 + recv2[zz, sr : sr + tr].astype(F32))
            return a, b

        stage3 = []
        for dz in (2, 1, 3):
            zz = lax.rem(z + dz, 4)
            a, b = sum2(zz)
            send3[dz - 1, 0:sr] = a.astype(BF16)
            send3[dz - 1, sr : sr + tr] = b.astype(BF16)
            copy = remote(send3.at[dz - 1], recv3.at[dz - 1], sem3.at[dz - 1], rsem3.at[dz - 1],
                          lax.rem(me + 4 * dz, n))
            copy.start()
            stage3.append(copy)
        for k in range(half, CHUNKS):
            back(k)
        a, b = sum2(z)
        for copy in stage3:
            copy.wait_recv()
        for slot in range(3):
            a = a + recv3[slot, 0:sr].astype(F32)
            b = b + recv3[slot, sr : sr + tr].astype(F32)
        sg[...] = a * g_scale
        tg[...] = b * g_scale
        ends = [pltpu.make_async_copy(sg, sg_hbm, local_sem.at[0]),
                pltpu.make_async_copy(tg, tg_hbm, local_sem.at[1])]
        for copy in ends:
            copy.start()
        for copy in stage1 + [stage2] + stage3:
            copy.wait_send()
    else:
        ends = [pltpu.make_async_copy(s_sum, sg_hbm, local_sem.at[0]),
                pltpu.make_async_copy(t_sum, tg_hbm, local_sem.at[1])]
        for copy in ends:
            copy.start()
        for k in range(CHUNKS):
            back(k)

    for k in range(CHUNKS):
        for has, copy in ((x_has_one, x_one), (x_has_two, x_two), (x_has_pass, x_pass),
                          (v_has_one, v_one), (v_has_two, v_two), (v_has_pass, v_pass)):
            @pl.when(has)
            def _():
                copy(k).wait_send()
        pltpu.make_async_copy(out_v.at[rows(k)], out_hbm.at[rows(k)], out_sem.at[k]).wait()
    for copy in ends:
        copy.wait()


def body(n, frames_in, cotangent, spatial_w, temporal_w):
    resident, height, cols, chans = frames_in.shape
    cells = resident * height * cols
    g_scale = 1.0 / math.sqrt(n * cells)
    sr, tr = 9 * chans // n, 3 * chans // n
    fused = n == 16 and sr % 16 == 0 and tr % 16 == 0
    both = sr + tr
    dma = pltpu.SemaphoreType.DMA
    scratch = [
        pltpu.VMEM((3, cells + 2 * cols, chans), BF16),
        pltpu.VMEM((3, 3, chans, chans), BF16),
        pltpu.VMEM((3, chans, chans), BF16),
        pltpu.VMEM((3, cells, chans), BF16),
        pltpu.VMEM((3, cells, chans), BF16),
        pltpu.VMEM((cells, chans), F32),
        pltpu.VMEM((chans, cells // CHUNKS), BF16),
        pltpu.VMEM((3 * chans, cells // CHUNKS), BF16),
        pltpu.VMEM((9 * chans, chans), F32),
        pltpu.VMEM((3 * chans, chans), F32),
        pltpu.VMEM((cells, chans), BF16),
        dma((4,)), dma((CHUNKS,)),
        dma((2, CHUNKS)), dma((CHUNKS,)), dma((2, CHUNKS)),
        dma((2, CHUNKS)), dma((CHUNKS,)), dma((2, CHUNKS)),
    ]
    if fused:
        scratch += [
            pltpu.VMEM((2, 4, both, chans), BF16), pltpu.VMEM((2, 4, both, chans), BF16),
            pltpu.VMEM((4, both, chans), BF16), pltpu.VMEM((4, both, chans), BF16),
            pltpu.VMEM((3, both, chans), BF16), pltpu.VMEM((3, both, chans), BF16),
            pltpu.VMEM((sr, chans), F32), pltpu.VMEM((tr, chans), F32),
            dma((2,)), dma((2,)), dma((1,)), dma((1,)), dma((3,)), dma((3,)),
        ]
    else:
        sr, tr = 9 * chans, 3 * chans
    anywhere = pl.BlockSpec(memory_space=pl.ANY)
    input_grad, sg, tg = pl.pallas_call(
        functools.partial(kernel, n, cells, cols, chans, fused, g_scale),
        out_shape=(
            jax.ShapeDtypeStruct((cells, chans), BF16),
            jax.ShapeDtypeStruct((sr, chans), F32),
            jax.ShapeDtypeStruct((tr, chans), F32),
        ),
        in_specs=[anywhere] * 4,
        out_specs=(anywhere,) * 3,
        scratch_shapes=scratch,
        compiler_params=pltpu.CompilerParams(
            collective_id=0, has_side_effects=True, vmem_limit_bytes=56 * 1024 * 1024
        ),
    )(frames_in.reshape(cells, chans), cotangent.reshape(cells, chans), spatial_w, temporal_w)
    if not fused:
        sg = lax.psum_scatter(sg, "ta", scatter_dimension=0, tiled=True) * g_scale
        tg = lax.psum_scatter(tg, "ta", scatter_dimension=0, tiled=True) * g_scale
    return input_grad.reshape(frames_in.shape), sg, tg


def solution(mesh):
    n = mesh.shape["ta"]
    in_specs = (P(("grp", "ta"), None, None, None), P(("grp", "ta"), None, None, None), P(), P())
    out_specs = (P(("grp", "ta"), None, None, None), P(("grp", "ta"), None), P(("grp", "ta"), None))
    return jax.shard_map(
        functools.partial(body, n), mesh=mesh, in_specs=in_specs, out_specs=out_specs,
        check_vma=False,
    )
```

```python
import functools
import math

import jax
import jax.numpy as jnp
from jax import lax
from jax.experimental import pallas as pl
from jax.experimental.pallas import tpu as pltpu
from jax.sharding import PartitionSpec as P

F32, BF16 = jnp.float32, jnp.bfloat16
CHUNKS = 4


def dot(a, b):
    return jnp.dot(a, b, preferred_element_type=F32)


def dot_t(a, b):
    return lax.dot_general(a, b, (((1,), (1,)), ((), ())), preferred_element_type=F32)


def kernel(
    n, cells, cols, chans,
    x_hbm, cot_hbm, sw_hbm, tw_hbm, *rest,
):
    out_hbm, sg_hbm, tg_hbm = rest[:3]
    (cotp, sw, tw, xs, vgs, agrad, act_t, x_t, s_sum, t_sum, out_v,
     local_sem, out_sem, xsend, xfwd, xrecv, vsend, vfwd, vrecv) = rest[3:]
    me = lax.axis_index("ta")
    core = lax.rem(me, 2)
    even = core == 0
    size = cells // CHUNKS

    def rows(k):
        return pl.ds(pl.multiple_of(k * size, size), size)

    def remote(src, dst, ssem, rsem, to):
        return pltpu.make_async_remote_copy(
            src_ref=src, dst_ref=dst, send_sem=ssem, recv_sem=rsem,
            device_id={"ta": to}, device_id_type=pl.DeviceIdType.MESH,
        )

    steps = [1, 2, n - 1, n - 2]
    barrier = pltpu.get_barrier_semaphore()
    for step in steps:
        pl.semaphore_signal(
            barrier, inc=1, device_id={"ta": lax.rem(me + step, n)},
            device_id_type=pl.DeviceIdType.MESH,
        )
    loads = [
        pltpu.make_async_copy(cot_hbm, cotp.at[1, pl.ds(cols, cells)], local_sem.at[0]),
        pltpu.make_async_copy(sw_hbm, sw, local_sem.at[1]),
        pltpu.make_async_copy(x_hbm, xs.at[0], local_sem.at[2]),
        pltpu.make_async_copy(tw_hbm, tw, local_sem.at[3]),
    ]
    for load in loads:
        load.start()
    pl.semaphore_wait(barrier, len(steps))

    def x_one(k):
        return remote(x_hbm.at[rows(k)], xs.at[1, rows(k)], xsend.at[0, k], xrecv.at[0, k],
                      lax.rem(me + 1, n))

    def x_two(k):
        return remote(x_hbm.at[rows(k)], xs.at[2, rows(k)], xsend.at[1, k], xrecv.at[1, k],
                      lax.rem(me + 2, n))

    def x_pass(k):
        return remote(xs.at[1, rows(k)], xs.at[2, rows(k)], xfwd.at[k], xrecv.at[1, k],
                      lax.rem(me + 1, n))

    def v_one(k):
        return remote(vgs.at[0, rows(k)], vgs.at[1, rows(k)], vsend.at[0, k], vrecv.at[0, k],
                      lax.rem(me + n - 1, n))

    def v_two(k):
        return remote(vgs.at[0, rows(k)], vgs.at[2, rows(k)], vsend.at[1, k], vrecv.at[1, k],
                      lax.rem(me + n - 2, n))

    def v_pass(k):
        return remote(vgs.at[1, rows(k)], vgs.at[2, rows(k)], vfwd.at[k], vrecv.at[1, k],
                      lax.rem(me + n - 1, n))

    x_has_one, x_has_two = me < n - 1, jnp.logical_and(even, me < n - 2)
    x_has_pass = jnp.logical_and(even, me >= 2)
    v_has_one, v_has_two = me >= 1, jnp.logical_and(core == 1, me >= 2)
    v_has_pass = jnp.logical_and(core == 1, me < n - 1)

    for k in range(CHUNKS):
        @pl.when(x_has_one)
        def _():
            x_one(k).start()

        @pl.when(x_has_two)
        def _():
            x_two(k).start()

    @pl.when(me == 0)
    def _():
        xs[1] = jnp.zeros((cells, chans), BF16)

    @pl.when(me < 2)
    def _():
        xs[2] = jnp.zeros((cells, chans), BF16)

    @pl.when(me == n - 1)
    def _():
        vgs[1] = jnp.zeros((cells, chans), BF16)

    @pl.when(me >= n - 2)
    def _():
        vgs[2] = jnp.zeros((cells, chans), BF16)

    edge = jnp.zeros((cols, chans), BF16)
    for j in range(3):
        cotp[j, pl.ds(0, cols)] = edge
        cotp[j, pl.ds(cols + cells, cols)] = edge
    loads[0].wait()

    def shift(k, carry):
        at = pl.ds(pl.multiple_of(cols + k * size, cols), size)
        piece = cotp[1, at].astype(F32)
        col = lax.rem(lax.broadcasted_iota(jnp.int32, (size, chans), 0), cols)
        cotp[0, at] = jnp.where(col == cols - 1, 0.0, pltpu.roll(piece, size - 1, 0)).astype(BF16)
        cotp[2, at] = jnp.where(col == 0, 0.0, pltpu.roll(piece, 1, 0)).astype(BF16)
        return carry

    lax.fori_loop(0, CHUNKS, shift, 0)
    loads[1].wait()

    def cot_at(k, i, j):
        return cotp[j, pl.ds(pl.multiple_of(k * size + (2 - i) * cols, cols), size)]

    def adjoint(k, carry):
        total = jnp.zeros((size, chans), F32)
        for i in range(3):
            for j in range(3):
                total = total + dot_t(cot_at(k, i, j), sw[i, j])
        agrad[rows(k)] = total
        return carry

    lax.fori_loop(0, CHUNKS, adjoint, 0)
    loads[2].wait()
    loads[3].wait()
    s_sum[...] = jnp.zeros_like(s_sum)
    t_sum[...] = jnp.zeros_like(t_sum)

    def send_v(k):
        @pl.when(v_has_one)
        def _():
            v_one(k).start()

        @pl.when(v_has_two)
        def _():
            v_two(k).start()

    def forward(k, carry):
        @pl.when(me >= 1)
        def _():
            x_one(k).wait_recv()

        @pl.when(x_has_pass)
        def _():
            x_pass(k).start()

        @pl.when(me >= 2)
        def _():
            x_two(k).wait_recv()

        at = rows(k)
        v = dot(xs[0, at], tw[0]) + dot(xs[1, at], tw[1]) + dot(xs[2, at], tw[2])
        s = 1.0 / (1.0 + jnp.exp(-v))
        vg = (agrad[at] * s * (1.0 + v * (1.0 - s))).astype(BF16)
        vgs[0, at] = vg
        act_t[...] = (v * s).astype(BF16).T
        for tap in range(3):
            x_t[tap * chans : (tap + 1) * chans] = xs[tap, at].T
        t_sum[...] += dot(x_t[...], vgs[0, at])
        for i in range(3):
            for j in range(3):
                block = pl.ds((3 * i + j) * chans, chans)
                s_sum[block] += dot(act_t[...], cot_at(k, i, j))
        return carry

    lax.fori_loop(0, CHUNKS, forward, 0)
    for k in range(CHUNKS):
        send_v(k)

    def back(k):
        @pl.when(me < n - 1)
        def _():
            v_one(k).wait_recv()

        @pl.when(v_has_pass)
        def _():
            v_pass(k).start()

        at = rows(k)
        total = dot_t(vgs[0, at], tw[0]) + dot_t(vgs[1, at], tw[1])

        @pl.when(me < n - 2)
        def _():
            v_two(k).wait_recv()

        total = total + dot_t(vgs[2, at], tw[2])
        cot = cotp[1, pl.ds(pl.multiple_of(cols + k * size, cols), size)].astype(F32)
        out_v[at] = (cot + total).astype(BF16)
        pltpu.make_async_copy(out_v.at[at], out_hbm.at[at], out_sem.at[k]).start()

    ends = [pltpu.make_async_copy(s_sum, sg_hbm, local_sem.at[0]),
            pltpu.make_async_copy(t_sum, tg_hbm, local_sem.at[1])]
    for copy in ends:
        copy.start()
    for k in range(CHUNKS):
        back(k)

    for k in range(CHUNKS):
        for has, copy in ((x_has_one, x_one), (x_has_two, x_two), (x_has_pass, x_pass),
                          (v_has_one, v_one), (v_has_two, v_two), (v_has_pass, v_pass)):
            @pl.when(has)
            def _():
                copy(k).wait_send()
        pltpu.make_async_copy(out_v.at[rows(k)], out_hbm.at[rows(k)], out_sem.at[k]).wait()
    for copy in ends:
        copy.wait()


def plane_kernel(
    n, cells, cols, chans, g_scale,
    x_hbm, cot_hbm, sw_hbm, tw_hbm, out_hbm, sg_hbm, tg_hbm,
    cotp, sw, tw, xs, vgs, agrad, act_t, x_t, s_sum, t_sum, out_v, cot_v, back_v, home_v,
    send1, recv1, send2, recv2, send3, recv3, sg, tg,
    local_sem, out_sem, xsend, xrecv, hsend, csend, crecv, rsend, rrecv, esend, erecv,
    vsend, vrecv, bsend, brecv, sem1, rsem1, sem2, rsem2, sem3, rsem3,
):
    me = lax.axis_index("ta")
    planes = n // 4
    z, q = me // 4, lax.rem(me, 4)
    y, core = q // 2, lax.rem(q, 2)
    base = me - q
    mate = me + 1 - 2 * core
    size = cells // 4
    deep = size + 2 * cols
    inner = pl.ds(cols, size)

    def rows(k):
        return pl.ds(pl.multiple_of(k * size, size), size)

    def near(s):
        return 2 * y + lax.rem(core + s, 2)

    def far(s):
        return 2 * (1 - y) + lax.rem(core + s, 2)

    def remote(src, dst, ssem, rsem, to):
        return pltpu.make_async_remote_copy(
            src_ref=src, dst_ref=dst, send_sem=ssem, recv_sem=rsem,
            device_id={"ta": to}, device_id_type=pl.DeviceIdType.MESH,
        )

    partners = [mate, base + far(0), base + far(1)]
    partners += [lax.rem(me + 4 * dz, n) for dz in range(1, planes)]
    barrier = pltpu.get_barrier_semaphore()
    for to in partners:
        pl.semaphore_signal(
            barrier, inc=1, device_id={"ta": to}, device_id_type=pl.DeviceIdType.MESH
        )
    has_top = q == 2
    has_bottom = q == 1
    row_above = pl.ds((cells // 2) - cols, cols)
    row_below = pl.ds(cells // 2, cols)
    loads = [
        pltpu.make_async_copy(cot_hbm.at[rows(q)], cotp.at[1, q, inner], local_sem.at[0]),
        pltpu.make_async_copy(sw_hbm, sw, local_sem.at[1]),
        pltpu.make_async_copy(x_hbm.at[rows(q)], xs.at[2 + q], local_sem.at[2]),
        pltpu.make_async_copy(tw_hbm, tw, local_sem.at[3]),
        pltpu.make_async_copy(cot_hbm, cot_v, local_sem.at[4]),
    ]
    for load in loads:
        load.start()
    top = pltpu.make_async_copy(
        cot_hbm.at[row_above], cotp.at[1, q, pl.ds(0, cols)], local_sem.at[5])
    bottom = pltpu.make_async_copy(
        cot_hbm.at[row_below], cotp.at[1, q, pl.ds(cols + size, cols)], local_sem.at[5])

    @pl.when(has_top)
    def _():
        top.start()

    @pl.when(has_bottom)
    def _():
        bottom.start()

    pl.semaphore_wait(barrier, len(partners))

    dests = [far(0), far(1), near(1)]

    def x_send(slot, to):
        return remote(x_hbm.at[rows(to)], xs.at[2 + q], xsend.at[slot], xrecv.at[2 + q], base + to)

    def cot_send(slot, to):
        return remote(cot_hbm.at[rows(to)], cotp.at[1, q, inner], csend.at[slot],
                      crecv.at[q], base + to)

    def top_send(f):
        return remote(cot_hbm.at[row_above], cotp.at[1, f, pl.ds(0, cols)], rsend.at[0],
                      rrecv.at[f], base + 2)

    def bottom_send(f):
        return remote(cot_hbm.at[row_below], cotp.at[1, f, pl.ds(cols + size, cols)],
                      rsend.at[1], rrecv.at[f], base + 1)

    def edge_down(f):
        return remote(cotp.at[1, f, pl.ds(size, cols)], cotp.at[1, f, pl.ds(0, cols)],
                      esend.at[f], erecv.at[f], mate)

    def edge_up(f):
        return remote(cotp.at[1, f, pl.ds(cols, cols)], cotp.at[1, f, pl.ds(cols + size, cols)],
                      esend.at[f], erecv.at[f], mate)

    def x_halo(i):
        return remote(xs.at[4 + i], xs.at[i], hsend.at[i], xrecv.at[i], lax.rem(me + 4, n))

    def v_halo(i):
        return remote(vgs.at[i], vgs.at[4 + i], vsend.at[i], vrecv.at[i],
                      lax.rem(me + n - 4, n))

    def b_send(f):
        return remote(back_v.at[f], home_v.at[rows(q)], bsend.at[f], brecv.at[q], base + f)

    for slot, to in enumerate(dests):
        x_send(slot, to).start()
    cot_send(2, dests[2]).start()

    @pl.when(q != 2)
    def _():
        top_send(q).start()

    @pl.when(q != 1)
    def _():
        bottom_send(q).start()

    for slot in range(2):
        cot_send(slot, dests[slot]).start()

    none = jnp.zeros((size, chans), BF16)
    edge = jnp.zeros((cols, chans), BF16)

    @pl.when(z == 0)
    def _():
        xs[0] = none
        xs[1] = none

    @pl.when(z == planes - 1)
    def _():
        vgs[4] = none
        vgs[5] = none

    @pl.when(q == 0)
    def _():
        for f in range(4):
            cotp[1, f, pl.ds(0, cols)] = edge

    @pl.when(q == 3)
    def _():
        for f in range(4):
            cotp[1, f, pl.ds(cols + size, cols)] = edge

    loads[2].wait()

    def pass_frames():
        for f in (2, 3):
            @pl.when(q != f)
            def _():
                remote(xs.at[2 + f], xs.at[2 + f], xsend.at[0], xrecv.at[2 + f], mate).wait_recv()

            @pl.when(z < planes - 1)
            def _():
                x_halo(f - 2).start()

    @pl.when(y == 1)
    def _():
        pass_frames()

    def trade_edges(f):
        @pl.when(core == 0)
        def _():
            edge_down(f).start()

        @pl.when(core == 1)
        def _():
            edge_up(f).start()

    def cot_arrives(f):
        remote(cotp.at[1, f, inner], cotp.at[1, f, inner], csend.at[0], crecv.at[f],
               mate).wait_recv()

    def shift(f):
        edge_down(f).wait_recv()
        piece = cotp[1, f].astype(F32)
        col = lax.rem(lax.broadcasted_iota(jnp.int32, (deep, chans), 0), cols)
        cotp[0, f] = jnp.where(col == cols - 1, 0.0, pltpu.roll(piece, deep - 1, 0)).astype(BF16)
        cotp[2, f] = jnp.where(col == 0, 0.0, pltpu.roll(piece, 1, 0)).astype(BF16)

    def cot_at(f, i, j):
        return cotp[j, f, pl.ds((2 - i) * cols, size)]

    def adjoint(f):
        total = jnp.zeros((size, chans), F32)
        for i in range(3):
            for j in range(3):
                total = total + dot_t(cot_at(f, i, j), sw[i, j])
        agrad[f] = total

    def cross_row(f):
        @pl.when(jnp.logical_or(has_top, has_bottom))
        def _():
            top_send(f).wait_recv()

    loads[0].wait()
    trade_edges(q)
    cot_arrives(near(1))
    trade_edges(near(1))

    @pl.when(has_top)
    def _():
        top.wait()

    @pl.when(has_bottom)
    def _():
        bottom.wait()

    cross_row(near(1))
    loads[1].wait()
    s_sum[...] = jnp.zeros_like(s_sum)
    t_sum[...] = jnp.zeros_like(t_sum)

    def local_adjoint(s, carry):
        shift(near(s))
        adjoint(near(s))
        return carry

    lax.fori_loop(0, 2, local_adjoint, 0)

    @pl.when(y == 0)
    def _():
        pass_frames()

    for f in (0, 1):
        @pl.when(q != f)
        def _():
            remote(xs.at[2 + f], xs.at[2 + f], xsend.at[0], xrecv.at[2 + f], mate).wait_recv()
    loads[3].wait()

    @pl.when(z > 0)
    def _():
        for i in range(2):
            x_halo(i).wait_recv()

    def forward(f):
        v = dot(xs[2 + f], tw[0]) + dot(xs[1 + f], tw[1]) + dot(xs[f], tw[2])
        s = 1.0 / (1.0 + jnp.exp(-v))
        vg = (agrad[f] * s * (1.0 + v * (1.0 - s))).astype(BF16)
        vgs[f] = vg

        @pl.when(jnp.logical_and(z > 0, f < 2))
        def _():
            v_halo(f).start()

        act_t[...] = (v * s).astype(BF16).T
        for tap in range(3):
            x_t[tap * chans : (tap + 1) * chans] = xs[2 + f - tap].T
        t_sum[...] += dot(x_t[...], vgs[f])
        for i in range(3):
            for j in range(3):
                block = pl.ds((3 * i + j) * chans, chans)
                s_sum[block] += dot(act_t[...], cot_at(f, i, j))

    def local_forward(s, carry):
        forward(near(s))
        return carry

    lax.fori_loop(0, 2, local_forward, 0)
    for s in range(2):
        cot_arrives(far(s))
        trade_edges(far(s))
        cross_row(far(s))

    def far_forward(s, carry):
        shift(far(s))
        adjoint(far(s))
        forward(far(s))
        return carry

    lax.fori_loop(0, 2, far_forward, 0)

    def back(f):
        total = dot_t(vgs[f], tw[0]) + dot_t(vgs[f + 1], tw[1]) + dot_t(vgs[f + 2], tw[2])
        back_v[f] = total.astype(BF16)

        @pl.when(q == f)
        def _():
            home_v[rows(q)] = back_v[f]

        @pl.when(q != f)
        def _():
            b_send(f).start()

    sr = 9 * chans // n
    tr = 3 * chans // n

    def own(b):
        return (s_sum[pl.ds(pl.multiple_of(sr * b, 16), sr)],
                t_sum[pl.ds(pl.multiple_of(tr * b, 16), tr)])

    stage1 = []
    for part in range(2):
        to_y = 1 - y if part == 0 else y
        for zz in range(4):
            a, b = own(4 * zz + 2 * to_y + (1 - core))
            send1[part, zz, 0:sr] = a.astype(BF16)
            send1[part, zz, sr : sr + tr] = b.astype(BF16)
        copy = remote(send1.at[part], recv1.at[part], sem1.at[part], rsem1.at[part],
                      me + 1 - 2 * core)
        copy.start()
        stage1.append(copy)
    back(0)
    back(1)
    stage1[0].wait_recv()
    for zz in range(4):
        a, b = own(4 * zz + 2 * (1 - y) + core)
        send2[zz, 0:sr] = (a + recv1[0, zz, 0:sr].astype(F32)).astype(BF16)
        send2[zz, sr : sr + tr] = (b + recv1[0, zz, sr : sr + tr].astype(F32)).astype(BF16)
    stage2 = remote(send2, recv2, sem2.at[0], rsem2.at[0], me + 2 - 4 * y)
    stage2.start()
    for f in (2, 3):
        @pl.when(z < planes - 1)
        def _():
            v_halo(f - 2).wait_recv()

        back(f)
    stage1[1].wait_recv()
    stage2.wait_recv()

    def sum2(zz):
        a, b = own(4 * zz + 2 * y + core)
        a = a + recv1[1, zz, 0:sr].astype(F32) + recv2[zz, 0:sr].astype(F32)
        b = (b + recv1[1, zz, sr : sr + tr].astype(F32)
             + recv2[zz, sr : sr + tr].astype(F32))
        return a, b

    stage3 = []
    for dz in (2, 1, 3):
        zz = lax.rem(z + dz, planes)
        a, b = sum2(zz)
        send3[dz - 1, 0:sr] = a.astype(BF16)
        send3[dz - 1, sr : sr + tr] = b.astype(BF16)
        copy = remote(send3.at[dz - 1], recv3.at[dz - 1], sem3.at[dz - 1], rsem3.at[dz - 1],
                      lax.rem(me + 4 * dz, n))
        copy.start()
        stage3.append(copy)
    loads[4].wait()
    for r in range(4):
        @pl.when(q != r)
        def _():
            remote(home_v.at[rows(r)], home_v.at[rows(r)], bsend.at[0], brecv.at[r],
                   mate).wait_recv()

        at = rows(r)
        out_v[at] = (cot_v[at].astype(F32) + home_v[at].astype(F32)).astype(BF16)
        pltpu.make_async_copy(out_v.at[at], out_hbm.at[at], out_sem.at[r]).start()
    a, b = sum2(z)
    for copy in stage3:
        copy.wait_recv()
    for slot in range(3):
        a = a + recv3[slot, 0:sr].astype(F32)
        b = b + recv3[slot, sr : sr + tr].astype(F32)
    sg[...] = a * g_scale
    tg[...] = b * g_scale
    ends = [pltpu.make_async_copy(sg, sg_hbm, local_sem.at[0]),
            pltpu.make_async_copy(tg, tg_hbm, local_sem.at[1])]
    for copy in ends:
        copy.start()
    for copy in stage1 + [stage2] + stage3:
        copy.wait_send()
    for slot, to in enumerate(dests):
        x_send(slot, to).wait_send()
        cot_send(slot, to).wait_send()

    @pl.when(q != 2)
    def _():
        top_send(q).wait_send()

    @pl.when(q != 1)
    def _():
        bottom_send(q).wait_send()

    for i in range(2):
        @pl.when(z < planes - 1)
        def _():
            x_halo(i).wait_send()

        @pl.when(z > 0)
        def _():
            v_halo(i).wait_send()
    for f in range(4):
        edge_down(f).wait_send()

        @pl.when(q != f)
        def _():
            b_send(f).wait_send()

        pltpu.make_async_copy(out_v.at[rows(f)], out_hbm.at[rows(f)], out_sem.at[f]).wait()
    for copy in ends:
        copy.wait()


def body(n, frames_in, cotangent, spatial_w, temporal_w):
    resident, height, cols, chans = frames_in.shape
    cells = resident * height * cols
    g_scale = 1.0 / math.sqrt(n * cells)
    sr, tr = 9 * chans // n, 3 * chans // n
    fused = n == 16 and resident == 1 and height % 4 == 0 and sr % 16 == 0 and tr % 16 == 0
    both = sr + tr
    dma = pltpu.SemaphoreType.DMA
    scratch = [
        pltpu.VMEM((3, cells + 2 * cols, chans), BF16),
        pltpu.VMEM((3, 3, chans, chans), BF16),
        pltpu.VMEM((3, chans, chans), BF16),
        pltpu.VMEM((3, cells, chans), BF16),
        pltpu.VMEM((3, cells, chans), BF16),
        pltpu.VMEM((cells, chans), F32),
        pltpu.VMEM((chans, cells // CHUNKS), BF16),
        pltpu.VMEM((3 * chans, cells // CHUNKS), BF16),
        pltpu.VMEM((9 * chans, chans), F32),
        pltpu.VMEM((3 * chans, chans), F32),
        pltpu.VMEM((cells, chans), BF16),
        dma((4,)), dma((CHUNKS,)),
        dma((2, CHUNKS)), dma((CHUNKS,)), dma((2, CHUNKS)),
        dma((2, CHUNKS)), dma((CHUNKS,)), dma((2, CHUNKS)),
    ]
    if fused:
        size = cells // 4
        scratch = [
            pltpu.VMEM((3, 4, size + 2 * cols, chans), BF16),
            pltpu.VMEM((3, 3, chans, chans), BF16),
            pltpu.VMEM((3, chans, chans), BF16),
            pltpu.VMEM((6, size, chans), BF16),
            pltpu.VMEM((6, size, chans), BF16),
            pltpu.VMEM((4, size, chans), F32),
            pltpu.VMEM((chans, size), BF16),
            pltpu.VMEM((3 * chans, size), BF16),
            pltpu.VMEM((9 * chans, chans), F32),
            pltpu.VMEM((3 * chans, chans), F32),
            pltpu.VMEM((cells, chans), BF16),
            pltpu.VMEM((cells, chans), BF16),
            pltpu.VMEM((4, size, chans), BF16),
            pltpu.VMEM((cells, chans), BF16),
            pltpu.VMEM((2, 4, both, chans), BF16), pltpu.VMEM((2, 4, both, chans), BF16),
            pltpu.VMEM((4, both, chans), BF16), pltpu.VMEM((4, both, chans), BF16),
            pltpu.VMEM((3, both, chans), BF16), pltpu.VMEM((3, both, chans), BF16),
            pltpu.VMEM((sr, chans), F32), pltpu.VMEM((tr, chans), F32),
            dma((6,)), dma((4,)), dma((3,)), dma((6,)), dma((2,)), dma((3,)), dma((4,)),
            dma((2,)), dma((4,)), dma((4,)), dma((4,)), dma((2,)), dma((2,)), dma((4,)), dma((4,)),
            dma((2,)), dma((2,)), dma((1,)), dma((1,)), dma((3,)), dma((3,)),
        ]
        step = functools.partial(plane_kernel, n, cells, cols, chans, g_scale)
    else:
        sr, tr = 9 * chans, 3 * chans
        step = functools.partial(kernel, n, cells, cols, chans)
    anywhere = pl.BlockSpec(memory_space=pl.ANY)
    input_grad, sg, tg = pl.pallas_call(
        step,
        out_shape=(
            jax.ShapeDtypeStruct((cells, chans), BF16),
            jax.ShapeDtypeStruct((sr, chans), F32),
            jax.ShapeDtypeStruct((tr, chans), F32),
        ),
        in_specs=[anywhere] * 4,
        out_specs=(anywhere,) * 3,
        scratch_shapes=scratch,
        compiler_params=pltpu.CompilerParams(
            collective_id=0 if fused else 1, has_side_effects=True, vmem_limit_bytes=56 * 1024 * 1024
        ),
    )(frames_in.reshape(cells, chans), cotangent.reshape(cells, chans), spatial_w, temporal_w)
    if not fused:
        sg = lax.psum_scatter(sg, "ta", scatter_dimension=0, tiled=True) * g_scale
        tg = lax.psum_scatter(tg, "ta", scatter_dimension=0, tiled=True) * g_scale
    return input_grad.reshape(frames_in.shape), sg, tg


def solution(mesh):
    n = mesh.shape["ta"]
    in_specs = (P(("grp", "ta"), None, None, None), P(("grp", "ta"), None, None, None), P(), P())
    out_specs = (P(("grp", "ta"), None, None, None), P(("grp", "ta"), None), P(("grp", "ta"), None))
    return jax.shard_map(
        functools.partial(body, n), mesh=mesh, in_specs=in_specs, out_specs=out_specs,
        check_vma=False,
    )
```

```python
import functools
import math

import jax
import jax.numpy as jnp
from jax import lax
from jax.experimental import pallas as pl
from jax.experimental.pallas import tpu as pltpu
from jax.sharding import PartitionSpec as P

F32, BF16 = jnp.float32, jnp.bfloat16
CHUNKS = 4


def dot(a, b):
    return jnp.dot(a, b, preferred_element_type=F32)


def dot_t(a, b):
    return lax.dot_general(a, b, (((1,), (1,)), ((), ())), preferred_element_type=F32)


def kernel(
    n, cells, cols, chans,
    x_hbm, cot_hbm, sw_hbm, tw_hbm, *rest,
):
    out_hbm, sg_hbm, tg_hbm = rest[:3]
    (cotp, sw, tw, xs, vgs, agrad, act_t, x_t, s_sum, t_sum, out_v,
     local_sem, out_sem, xsend, xfwd, xrecv, vsend, vfwd, vrecv) = rest[3:]
    me = lax.axis_index("ta")
    core = lax.rem(me, 2)
    even = core == 0
    size = cells // CHUNKS

    def rows(k):
        return pl.ds(pl.multiple_of(k * size, size), size)

    def remote(src, dst, ssem, rsem, to):
        return pltpu.make_async_remote_copy(
            src_ref=src, dst_ref=dst, send_sem=ssem, recv_sem=rsem,
            device_id={"ta": to}, device_id_type=pl.DeviceIdType.MESH,
        )

    steps = [1, 2, n - 1, n - 2]
    barrier = pltpu.get_barrier_semaphore()
    for step in steps:
        pl.semaphore_signal(
            barrier, inc=1, device_id={"ta": lax.rem(me + step, n)},
            device_id_type=pl.DeviceIdType.MESH,
        )
    loads = [
        pltpu.make_async_copy(cot_hbm, cotp.at[1, pl.ds(cols, cells)], local_sem.at[0]),
        pltpu.make_async_copy(sw_hbm, sw, local_sem.at[1]),
        pltpu.make_async_copy(x_hbm, xs.at[0], local_sem.at[2]),
        pltpu.make_async_copy(tw_hbm, tw, local_sem.at[3]),
    ]
    for load in loads:
        load.start()
    pl.semaphore_wait(barrier, len(steps))

    def x_one(k):
        return remote(x_hbm.at[rows(k)], xs.at[1, rows(k)], xsend.at[0, k], xrecv.at[0, k],
                      lax.rem(me + 1, n))

    def x_two(k):
        return remote(x_hbm.at[rows(k)], xs.at[2, rows(k)], xsend.at[1, k], xrecv.at[1, k],
                      lax.rem(me + 2, n))

    def x_pass(k):
        return remote(xs.at[1, rows(k)], xs.at[2, rows(k)], xfwd.at[k], xrecv.at[1, k],
                      lax.rem(me + 1, n))

    def v_one(k):
        return remote(vgs.at[0, rows(k)], vgs.at[1, rows(k)], vsend.at[0, k], vrecv.at[0, k],
                      lax.rem(me + n - 1, n))

    def v_two(k):
        return remote(vgs.at[0, rows(k)], vgs.at[2, rows(k)], vsend.at[1, k], vrecv.at[1, k],
                      lax.rem(me + n - 2, n))

    def v_pass(k):
        return remote(vgs.at[1, rows(k)], vgs.at[2, rows(k)], vfwd.at[k], vrecv.at[1, k],
                      lax.rem(me + n - 1, n))

    x_has_one, x_has_two = me < n - 1, jnp.logical_and(even, me < n - 2)
    x_has_pass = jnp.logical_and(even, me >= 2)
    v_has_one, v_has_two = me >= 1, jnp.logical_and(core == 1, me >= 2)
    v_has_pass = jnp.logical_and(core == 1, me < n - 1)

    for k in range(CHUNKS):
        @pl.when(x_has_one)
        def _():
            x_one(k).start()

        @pl.when(x_has_two)
        def _():
            x_two(k).start()

    @pl.when(me == 0)
    def _():
        xs[1] = jnp.zeros((cells, chans), BF16)

    @pl.when(me < 2)
    def _():
        xs[2] = jnp.zeros((cells, chans), BF16)

    @pl.when(me == n - 1)
    def _():
        vgs[1] = jnp.zeros((cells, chans), BF16)

    @pl.when(me >= n - 2)
    def _():
        vgs[2] = jnp.zeros((cells, chans), BF16)

    edge = jnp.zeros((cols, chans), BF16)
    for j in range(3):
        cotp[j, pl.ds(0, cols)] = edge
        cotp[j, pl.ds(cols + cells, cols)] = edge
    loads[0].wait()

    def shift(k, carry):
        at = pl.ds(pl.multiple_of(cols + k * size, cols), size)
        piece = cotp[1, at].astype(F32)
        col = lax.rem(lax.broadcasted_iota(jnp.int32, (size, chans), 0), cols)
        cotp[0, at] = jnp.where(col == cols - 1, 0.0, pltpu.roll(piece, size - 1, 0)).astype(BF16)
        cotp[2, at] = jnp.where(col == 0, 0.0, pltpu.roll(piece, 1, 0)).astype(BF16)
        return carry

    lax.fori_loop(0, CHUNKS, shift, 0)
    loads[1].wait()

    def cot_at(k, i, j):
        return cotp[j, pl.ds(pl.multiple_of(k * size + (2 - i) * cols, cols), size)]

    def adjoint(k, carry):
        total = jnp.zeros((size, chans), F32)
        for i in range(3):
            for j in range(3):
                total = total + dot_t(cot_at(k, i, j), sw[i, j])
        agrad[rows(k)] = total
        return carry

    lax.fori_loop(0, CHUNKS, adjoint, 0)
    loads[2].wait()
    loads[3].wait()
    s_sum[...] = jnp.zeros_like(s_sum)
    t_sum[...] = jnp.zeros_like(t_sum)

    def send_v(k):
        @pl.when(v_has_one)
        def _():
            v_one(k).start()

        @pl.when(v_has_two)
        def _():
            v_two(k).start()

    def forward(k, carry):
        @pl.when(me >= 1)
        def _():
            x_one(k).wait_recv()

        @pl.when(x_has_pass)
        def _():
            x_pass(k).start()

        @pl.when(me >= 2)
        def _():
            x_two(k).wait_recv()

        at = rows(k)
        v = dot(xs[0, at], tw[0]) + dot(xs[1, at], tw[1]) + dot(xs[2, at], tw[2])
        s = 1.0 / (1.0 + jnp.exp(-v))
        vg = (agrad[at] * s * (1.0 + v * (1.0 - s))).astype(BF16)
        vgs[0, at] = vg
        act_t[...] = (v * s).astype(BF16).T
        for tap in range(3):
            x_t[tap * chans : (tap + 1) * chans] = xs[tap, at].T
        t_sum[...] += dot(x_t[...], vgs[0, at])
        for i in range(3):
            for j in range(3):
                block = pl.ds((3 * i + j) * chans, chans)
                s_sum[block] += dot(act_t[...], cot_at(k, i, j))
        return carry

    lax.fori_loop(0, CHUNKS, forward, 0)
    for k in range(CHUNKS):
        send_v(k)

    def back(k):
        @pl.when(me < n - 1)
        def _():
            v_one(k).wait_recv()

        @pl.when(v_has_pass)
        def _():
            v_pass(k).start()

        at = rows(k)
        total = dot_t(vgs[0, at], tw[0]) + dot_t(vgs[1, at], tw[1])

        @pl.when(me < n - 2)
        def _():
            v_two(k).wait_recv()

        total = total + dot_t(vgs[2, at], tw[2])
        cot = cotp[1, pl.ds(pl.multiple_of(cols + k * size, cols), size)].astype(F32)
        out_v[at] = (cot + total).astype(BF16)
        pltpu.make_async_copy(out_v.at[at], out_hbm.at[at], out_sem.at[k]).start()

    ends = [pltpu.make_async_copy(s_sum, sg_hbm, local_sem.at[0]),
            pltpu.make_async_copy(t_sum, tg_hbm, local_sem.at[1])]
    for copy in ends:
        copy.start()
    for k in range(CHUNKS):
        back(k)

    for k in range(CHUNKS):
        for has, copy in ((x_has_one, x_one), (x_has_two, x_two), (x_has_pass, x_pass),
                          (v_has_one, v_one), (v_has_two, v_two), (v_has_pass, v_pass)):
            @pl.when(has)
            def _():
                copy(k).wait_send()
        pltpu.make_async_copy(out_v.at[rows(k)], out_hbm.at[rows(k)], out_sem.at[k]).wait()
    for copy in ends:
        copy.wait()


def plane_kernel(
    n, cells, cols, chans, g_scale,
    x_hbm, cot_hbm, sw_hbm, tw_hbm, out_hbm, sg_hbm, tg_hbm,
    cotp, sw, tw, xs, vgs, agrad, act_t, x_t, s_sum, t_sum, out_v, cot_v, back_v, home_v,
    send1, recv1, send2, recv2, send3, recv3, sg, tg,
    local_sem, out_sem, xsend, xrecv, hsend, csend, crecv, rsend, rrecv, esend, erecv,
    vsend, vrecv, bsend, brecv, sem1, rsem1, sem2, rsem2, sem3, rsem3,
):
    me = lax.axis_index("ta")
    planes = n // 4
    z, q = me // 4, lax.rem(me, 4)
    y, core = q // 2, lax.rem(q, 2)
    base = me - q
    mate = me + 1 - 2 * core
    size = cells // 4
    deep = size + 2 * cols
    inner = pl.ds(cols, size)

    def rows(k):
        return pl.ds(pl.multiple_of(k * size, size), size)

    def near(s):
        return 2 * y + lax.rem(core + s, 2)

    def far(s):
        return 2 * (1 - y) + lax.rem(core + s, 2)

    def remote(src, dst, ssem, rsem, to):
        return pltpu.make_async_remote_copy(
            src_ref=src, dst_ref=dst, send_sem=ssem, recv_sem=rsem,
            device_id={"ta": to}, device_id_type=pl.DeviceIdType.MESH,
        )

    partners = [mate, base + far(0), base + far(1)]
    partners += [lax.rem(me + 4 * dz, n) for dz in range(1, planes)]
    barrier = pltpu.get_barrier_semaphore()
    for to in partners:
        pl.semaphore_signal(
            barrier, inc=1, device_id={"ta": to}, device_id_type=pl.DeviceIdType.MESH
        )
    has_top = q == 2
    has_bottom = q == 1
    row_above = pl.ds((cells // 2) - cols, cols)
    row_below = pl.ds(cells // 2, cols)
    loads = [
        pltpu.make_async_copy(cot_hbm.at[rows(q)], cotp.at[1, q, inner], local_sem.at[0]),
        pltpu.make_async_copy(sw_hbm, sw, local_sem.at[1]),
        pltpu.make_async_copy(x_hbm.at[rows(q)], xs.at[2 + q], local_sem.at[2]),
        pltpu.make_async_copy(tw_hbm, tw, local_sem.at[3]),
        pltpu.make_async_copy(cot_hbm, cot_v, local_sem.at[4]),
    ]
    for load in loads:
        load.start()
    top = pltpu.make_async_copy(
        cot_hbm.at[row_above], cotp.at[1, q, pl.ds(0, cols)], local_sem.at[5])
    bottom = pltpu.make_async_copy(
        cot_hbm.at[row_below], cotp.at[1, q, pl.ds(cols + size, cols)], local_sem.at[5])

    @pl.when(has_top)
    def _():
        top.start()

    @pl.when(has_bottom)
    def _():
        bottom.start()

    pl.semaphore_wait(barrier, len(partners))

    dests = [far(0), far(1), near(1)]

    def x_send(slot, to):
        return remote(x_hbm.at[rows(to)], xs.at[2 + q], xsend.at[slot], xrecv.at[2 + q], base + to)

    def cot_send(slot, to):
        return remote(cot_hbm.at[rows(to)], cotp.at[1, q, inner], csend.at[slot],
                      crecv.at[q], base + to)

    def top_send(f):
        return remote(cot_hbm.at[row_above], cotp.at[1, f, pl.ds(0, cols)], rsend.at[0],
                      rrecv.at[f], base + 2)

    def bottom_send(f):
        return remote(cot_hbm.at[row_below], cotp.at[1, f, pl.ds(cols + size, cols)],
                      rsend.at[1], rrecv.at[f], base + 1)

    def edge_down(f):
        return remote(cotp.at[1, f, pl.ds(size, cols)], cotp.at[1, f, pl.ds(0, cols)],
                      esend.at[f], erecv.at[f], mate)

    def edge_up(f):
        return remote(cotp.at[1, f, pl.ds(cols, cols)], cotp.at[1, f, pl.ds(cols + size, cols)],
                      esend.at[f], erecv.at[f], mate)

    def x_halo(i):
        return remote(xs.at[4 + i], xs.at[i], hsend.at[i], xrecv.at[i], lax.rem(me + 4, n))

    def v_halo(i):
        return remote(vgs.at[i], vgs.at[4 + i], vsend.at[i], vrecv.at[i],
                      lax.rem(me + n - 4, n))

    def b_send(f):
        return remote(back_v.at[f], home_v.at[rows(q)], bsend.at[f], brecv.at[q], base + f)

    for slot, to in enumerate(dests):
        x_send(slot, to).start()
    cot_send(2, dests[2]).start()

    @pl.when(q != 2)
    def _():
        top_send(q).start()

    @pl.when(q != 1)
    def _():
        bottom_send(q).start()

    for slot in range(2):
        cot_send(slot, dests[slot]).start()

    none = jnp.zeros((size, chans), BF16)
    edge = jnp.zeros((cols, chans), BF16)

    @pl.when(z == 0)
    def _():
        xs[0] = none
        xs[1] = none

    @pl.when(z == planes - 1)
    def _():
        vgs[4] = none
        vgs[5] = none

    @pl.when(q == 0)
    def _():
        for f in range(4):
            cotp[1, f, pl.ds(0, cols)] = edge

    @pl.when(q == 3)
    def _():
        for f in range(4):
            cotp[1, f, pl.ds(cols + size, cols)] = edge

    loads[2].wait()

    def pass_frames():
        for f in (2, 3):
            @pl.when(q != f)
            def _():
                remote(xs.at[2 + f], xs.at[2 + f], xsend.at[0], xrecv.at[2 + f], mate).wait_recv()

            @pl.when(z < planes - 1)
            def _():
                x_halo(f - 2).start()

    @pl.when(y == 1)
    def _():
        pass_frames()

    def trade_edges(f):
        @pl.when(core == 0)
        def _():
            edge_down(f).start()

        @pl.when(core == 1)
        def _():
            edge_up(f).start()

    def cot_arrives(f):
        remote(cotp.at[1, f, inner], cotp.at[1, f, inner], csend.at[0], crecv.at[f],
               mate).wait_recv()

    def shift(f):
        edge_down(f).wait_recv()
        piece = cotp[1, f].astype(F32)
        col = lax.rem(lax.broadcasted_iota(jnp.int32, (deep, chans), 0), cols)
        cotp[0, f] = jnp.where(col == cols - 1, 0.0, pltpu.roll(piece, deep - 1, 0)).astype(BF16)
        cotp[2, f] = jnp.where(col == 0, 0.0, pltpu.roll(piece, 1, 0)).astype(BF16)

    def cot_at(f, i, j):
        return cotp[j, f, pl.ds((2 - i) * cols, size)]

    def adjoint(f):
        total = jnp.zeros((size, chans), F32)
        for i in range(3):
            for j in range(3):
                total = total + dot_t(cot_at(f, i, j), sw[i, j])
        agrad[f] = total

    def cross_row(f):
        @pl.when(jnp.logical_or(has_top, has_bottom))
        def _():
            top_send(f).wait_recv()

    loads[0].wait()
    trade_edges(q)
    cot_arrives(near(1))
    trade_edges(near(1))

    @pl.when(has_top)
    def _():
        top.wait()

    @pl.when(has_bottom)
    def _():
        bottom.wait()

    cross_row(near(1))
    loads[1].wait()
    s_sum[...] = jnp.zeros_like(s_sum)
    t_sum[...] = jnp.zeros_like(t_sum)

    def local_adjoint(s, carry):
        shift(near(s))
        adjoint(near(s))
        return carry

    lax.fori_loop(0, 2, local_adjoint, 0)

    @pl.when(y == 0)
    def _():
        pass_frames()

    for f in (0, 1):
        @pl.when(q != f)
        def _():
            remote(xs.at[2 + f], xs.at[2 + f], xsend.at[0], xrecv.at[2 + f], mate).wait_recv()
    loads[3].wait()

    @pl.when(z > 0)
    def _():
        for i in range(2):
            x_halo(i).wait_recv()

    def forward(f):
        v = dot(xs[2 + f], tw[0]) + dot(xs[1 + f], tw[1]) + dot(xs[f], tw[2])
        s = 1.0 / (1.0 + jnp.exp(-v))
        vg = (agrad[f] * s * (1.0 + v * (1.0 - s))).astype(BF16)
        vgs[f] = vg

        @pl.when(jnp.logical_and(z > 0, f < 2))
        def _():
            v_halo(f).start()

        act_t[...] = (v * s).astype(BF16).T
        for tap in range(3):
            x_t[tap * chans : (tap + 1) * chans] = xs[2 + f - tap].T
        t_sum[...] += dot(x_t[...], vgs[f])
        for i in range(3):
            for j in range(3):
                block = pl.ds((3 * i + j) * chans, chans)
                s_sum[block] += dot(act_t[...], cot_at(f, i, j))

    def local_forward(s, carry):
        forward(near(s))
        return carry

    lax.fori_loop(0, 2, local_forward, 0)
    for s in range(2):
        cot_arrives(far(s))
        trade_edges(far(s))
        cross_row(far(s))

    def far_forward(s, carry):
        shift(far(s))
        adjoint(far(s))
        forward(far(s))
        return carry

    lax.fori_loop(0, 2, far_forward, 0)

    def back(f):
        total = dot_t(vgs[f], tw[0]) + dot_t(vgs[f + 1], tw[1]) + dot_t(vgs[f + 2], tw[2])
        back_v[f] = total.astype(BF16)

        @pl.when(q == f)
        def _():
            home_v[rows(q)] = back_v[f]

        @pl.when(q != f)
        def _():
            b_send(f).start()

    sr = 9 * chans // n
    tr = 3 * chans // n

    def own(b):
        return (s_sum[pl.ds(pl.multiple_of(sr * b, 16), sr)],
                t_sum[pl.ds(pl.multiple_of(tr * b, 16), tr)])

    stage1 = []
    for part in range(2):
        to_y = 1 - y if part == 0 else y
        for zz in range(4):
            a, b = own(4 * zz + 2 * to_y + (1 - core))
            send1[part, zz, 0:sr] = a.astype(BF16)
            send1[part, zz, sr : sr + tr] = b.astype(BF16)
        copy = remote(send1.at[part], recv1.at[part], sem1.at[part], rsem1.at[part],
                      me + 1 - 2 * core)
        copy.start()
        stage1.append(copy)
    stage1[0].wait_recv()
    for zz in range(4):
        a, b = own(4 * zz + 2 * (1 - y) + core)
        send2[zz, 0:sr] = (a + recv1[0, zz, 0:sr].astype(F32)).astype(BF16)
        send2[zz, sr : sr + tr] = (b + recv1[0, zz, sr : sr + tr].astype(F32)).astype(BF16)
    stage2 = remote(send2, recv2, sem2.at[0], rsem2.at[0], me + 2 - 4 * y)
    stage2.start()
    back(0)
    back(1)
    for f in (2, 3):
        @pl.when(z < planes - 1)
        def _():
            v_halo(f - 2).wait_recv()

        back(f)
    stage1[1].wait_recv()
    stage2.wait_recv()

    def sum2(zz):
        a, b = own(4 * zz + 2 * y + core)
        a = a + recv1[1, zz, 0:sr].astype(F32) + recv2[zz, 0:sr].astype(F32)
        b = (b + recv1[1, zz, sr : sr + tr].astype(F32)
             + recv2[zz, sr : sr + tr].astype(F32))
        return a, b

    stage3 = []
    for dz in (2, 1, 3):
        zz = lax.rem(z + dz, planes)
        a, b = sum2(zz)
        send3[dz - 1, 0:sr] = a.astype(BF16)
        send3[dz - 1, sr : sr + tr] = b.astype(BF16)
        copy = remote(send3.at[dz - 1], recv3.at[dz - 1], sem3.at[dz - 1], rsem3.at[dz - 1],
                      lax.rem(me + 4 * dz, n))
        copy.start()
        stage3.append(copy)
    loads[4].wait()
    for r in range(4):
        @pl.when(q != r)
        def _():
            remote(home_v.at[rows(r)], home_v.at[rows(r)], bsend.at[0], brecv.at[r],
                   mate).wait_recv()

        at = rows(r)
        out_v[at] = (cot_v[at].astype(F32) + home_v[at].astype(F32)).astype(BF16)
        pltpu.make_async_copy(out_v.at[at], out_hbm.at[at], out_sem.at[r]).start()
    a, b = sum2(z)
    for copy in stage3:
        copy.wait_recv()
    for slot in range(3):
        a = a + recv3[slot, 0:sr].astype(F32)
        b = b + recv3[slot, sr : sr + tr].astype(F32)
    sg[...] = a * g_scale
    tg[...] = b * g_scale
    ends = [pltpu.make_async_copy(sg, sg_hbm, local_sem.at[0]),
            pltpu.make_async_copy(tg, tg_hbm, local_sem.at[1])]
    for copy in ends:
        copy.start()
    for copy in stage1 + [stage2] + stage3:
        copy.wait_send()
    for slot, to in enumerate(dests):
        x_send(slot, to).wait_send()
        cot_send(slot, to).wait_send()

    @pl.when(q != 2)
    def _():
        top_send(q).wait_send()

    @pl.when(q != 1)
    def _():
        bottom_send(q).wait_send()

    for i in range(2):
        @pl.when(z < planes - 1)
        def _():
            x_halo(i).wait_send()

        @pl.when(z > 0)
        def _():
            v_halo(i).wait_send()
    for f in range(4):
        edge_down(f).wait_send()

        @pl.when(q != f)
        def _():
            b_send(f).wait_send()

        pltpu.make_async_copy(out_v.at[rows(f)], out_hbm.at[rows(f)], out_sem.at[f]).wait()
    for copy in ends:
        copy.wait()


def body(n, frames_in, cotangent, spatial_w, temporal_w):
    resident, height, cols, chans = frames_in.shape
    cells = resident * height * cols
    g_scale = 1.0 / math.sqrt(n * cells)
    sr, tr = 9 * chans // n, 3 * chans // n
    fused = n == 16 and resident == 1 and height % 4 == 0 and sr % 16 == 0 and tr % 16 == 0
    both = sr + tr
    dma = pltpu.SemaphoreType.DMA
    scratch = [
        pltpu.VMEM((3, cells + 2 * cols, chans), BF16),
        pltpu.VMEM((3, 3, chans, chans), BF16),
        pltpu.VMEM((3, chans, chans), BF16),
        pltpu.VMEM((3, cells, chans), BF16),
        pltpu.VMEM((3, cells, chans), BF16),
        pltpu.VMEM((cells, chans), F32),
        pltpu.VMEM((chans, cells // CHUNKS), BF16),
        pltpu.VMEM((3 * chans, cells // CHUNKS), BF16),
        pltpu.VMEM((9 * chans, chans), F32),
        pltpu.VMEM((3 * chans, chans), F32),
        pltpu.VMEM((cells, chans), BF16),
        dma((4,)), dma((CHUNKS,)),
        dma((2, CHUNKS)), dma((CHUNKS,)), dma((2, CHUNKS)),
        dma((2, CHUNKS)), dma((CHUNKS,)), dma((2, CHUNKS)),
    ]
    if fused:
        size = cells // 4
        scratch = [
            pltpu.VMEM((3, 4, size + 2 * cols, chans), BF16),
            pltpu.VMEM((3, 3, chans, chans), BF16),
            pltpu.VMEM((3, chans, chans), BF16),
            pltpu.VMEM((6, size, chans), BF16),
            pltpu.VMEM((6, size, chans), BF16),
            pltpu.VMEM((4, size, chans), F32),
            pltpu.VMEM((chans, size), BF16),
            pltpu.VMEM((3 * chans, size), BF16),
            pltpu.VMEM((9 * chans, chans), F32),
            pltpu.VMEM((3 * chans, chans), F32),
            pltpu.VMEM((cells, chans), BF16),
            pltpu.VMEM((cells, chans), BF16),
            pltpu.VMEM((4, size, chans), BF16),
            pltpu.VMEM((cells, chans), BF16),
            pltpu.VMEM((2, 4, both, chans), BF16), pltpu.VMEM((2, 4, both, chans), BF16),
            pltpu.VMEM((4, both, chans), BF16), pltpu.VMEM((4, both, chans), BF16),
            pltpu.VMEM((3, both, chans), BF16), pltpu.VMEM((3, both, chans), BF16),
            pltpu.VMEM((sr, chans), F32), pltpu.VMEM((tr, chans), F32),
            dma((6,)), dma((4,)), dma((3,)), dma((6,)), dma((2,)), dma((3,)), dma((4,)),
            dma((2,)), dma((4,)), dma((4,)), dma((4,)), dma((2,)), dma((2,)), dma((4,)), dma((4,)),
            dma((2,)), dma((2,)), dma((1,)), dma((1,)), dma((3,)), dma((3,)),
        ]
        step = functools.partial(plane_kernel, n, cells, cols, chans, g_scale)
    else:
        sr, tr = 9 * chans, 3 * chans
        step = functools.partial(kernel, n, cells, cols, chans)
    anywhere = pl.BlockSpec(memory_space=pl.ANY)
    input_grad, sg, tg = pl.pallas_call(
        step,
        out_shape=(
            jax.ShapeDtypeStruct((cells, chans), BF16),
            jax.ShapeDtypeStruct((sr, chans), F32),
            jax.ShapeDtypeStruct((tr, chans), F32),
        ),
        in_specs=[anywhere] * 4,
        out_specs=(anywhere,) * 3,
        scratch_shapes=scratch,
        compiler_params=pltpu.CompilerParams(
            collective_id=0 if fused else 1, has_side_effects=True, vmem_limit_bytes=56 * 1024 * 1024
        ),
    )(frames_in.reshape(cells, chans), cotangent.reshape(cells, chans), spatial_w, temporal_w)
    if not fused:
        sg = lax.psum_scatter(sg, "ta", scatter_dimension=0, tiled=True) * g_scale
        tg = lax.psum_scatter(tg, "ta", scatter_dimension=0, tiled=True) * g_scale
    return input_grad.reshape(frames_in.shape), sg, tg


def solution(mesh):
    n = mesh.shape["ta"]
    in_specs = (P(("grp", "ta"), None, None, None), P(("grp", "ta"), None, None, None), P(), P())
    out_specs = (P(("grp", "ta"), None, None, None), P(("grp", "ta"), None), P(("grp", "ta"), None))
    return jax.shard_map(
        functools.partial(body, n), mesh=mesh, in_specs=in_specs, out_specs=out_specs,
        check_vma=False,
    )
```
